32 devices in a mesh: outer: 2 (over y), shard: 16 (over z, x, core).
Axes of the slice: x: 2, y: 2, z: 4, core: 2. Of those that a mesh axis runs over, the one named last changes fastest.
Arguments:
- grad_values: bfloat16 [2, 16, 256, 14848], P('outer', 'shard'), may hold values from -6 to 6
- grad_scales: bfloat16 [2, 16, 256, 116], P('outer', 'shard'), may hold values from 0.029907227 to 0.29882812
- block_owner: int32 [256], replicated, may hold values from 0 to 15, as said below
- projector: bfloat16 [8192, 256], P(('outer', 'shard')), may hold values from -0.375 to 0.375
- weights: bfloat16 [8192, 14848], P(('outer', 'shard')), may hold values from -6 to 6
- first_moment: float32 [256, 14848], P('shard'), may hold values from -6 to 6
- second_moment: float32 [256, 14848], P('shard'), may hold values from 0.5 to 4
Outputs:
- new_weights: bfloat16 [8192, 14848], P(('outer', 'shard'))
- new_first: float32 [256, 14848], P('shard')
- new_second: float32 [256, 14848], P('shard')
The draws below stay inside these ranges and needn't reach their ends.
Inputs may be any that keep to these rules, and one draw needn't show every extreme that they name: `block_owner`: every index of shard owns exactly 16 rows.
All inputs are finite; a program needn't handle non-finite values.
Results may differ from the reference program's by a relative error of at most 0.0015.
Values may be sent and summed in bfloat16 or wider, within the bound.
No kernel may reach another device: no remote copies, remote signals or barrier semaphores. Data moves between devices by JAX's collectives and lax.ppermute only.
A program may use at most 128 MiB of HBM per device.

```python
import math
import jax
import jax.numpy as jnp
from jax import lax

D = 8192
FFW = 14848
RANK = 256
BLOCK = 128
COL_BLOCKS = 116
ROWS_OWN = 16
N_OUTER = 2
N_SHARD = 16


def draw_block_owner(key, part):
    shuffled = jax.random.permutation(key, RANK)
    return (shuffled // ROWS_OWN).astype(jnp.int32)


def block_levels(key, dims, cuts, least, top_value):
    loudness, own = 1.0, jax.random.fold_in(key, 6)
    for position, parts in cuts:
        heights = jnp.exp(jax.random.uniform(jax.random.fold_in(own, position), (parts,), jnp.float32, least / len(cuts), top_value / len(cuts)))
        loudness = loudness * jnp.repeat(heights, dims[position] // parts).reshape([-1 if axis == position else 1 for axis in range(len(dims))])
    return loudness


def normal_values(rng, extent, scale, limit, shards=(), kind=jnp.bfloat16):
    array = jax.random.normal(rng, extent, jnp.float32) * scale
    if len(shards) > 0:
        array = block_levels(rng, extent, shards, -0.22, 0.18) * array
    return jnp.clip(array, min=-limit, max=limit).astype(kind)


def setup_inputs(seed: int = 0) -> dict:
    splits = jax.random.split(jax.random.key(seed), 8)
    return {
        "grad_values": normal_values(splits[0], (N_OUTER, N_SHARD, RANK, FFW), 1.0, 6.0, ((0, 2), (1, 16))),
        "grad_scales": jnp.clip(jnp.exp(math.log(0.29882812) - 2.30176843 * jax.random.uniform(splits[1], (N_OUTER, N_SHARD, RANK, COL_BLOCKS), jnp.float32) ** block_levels(splits[1], (N_OUTER, N_SHARD, RANK, COL_BLOCKS), ((0, 2), (1, 16)), -0.2, 0.2)), 0.029907227, 0.29882812).astype(jnp.bfloat16),
        "block_owner": draw_block_owner(jax.random.fold_in(splits[7], 71), 0),
        "projector": normal_values(splits[3], (D, RANK), RANK ** -0.5, 0.375, ((0, 32),)),
        "weights": normal_values(splits[4], (D, FFW), 1.0, 6.0, ((0, 32),)),
        "first_moment": normal_values(splits[5], (RANK, FFW), 1.0, 6.0, ((0, 16),), jnp.float32),
        "second_moment": jnp.clip(jnp.exp(math.log(4.0) - 2.0794415 * jax.random.uniform(splits[6], (RANK, FFW), jnp.float32) ** block_levels(splits[6], (RANK, FFW), ((0, 16),), -0.2, 0.2)), 0.5, 4.0),
    }


first_decay = 0.9
second_decay = 0.999
step_count = 100.0
update_scale = 0.25

def reference(grad_values, grad_scales, block_owner, projector, weights, first_moment, second_moment):
    row_order = jnp.argsort(block_owner * RANK + jnp.arange(RANK, dtype=jnp.int32)).astype(jnp.int32)
    inverse = jnp.argsort(row_order).astype(jnp.int32)

    def per_pod(pieces):
        values, scales = pieces
        blocked = values.astype(jnp.float32).reshape(N_SHARD, RANK, COL_BLOCKS, BLOCK)
        pod_sum = lax.optimization_barrier(jnp.sum(blocked * scales.astype(jnp.float32)[..., None], axis=0))
        pod_low = lax.optimization_barrier(pod_sum.astype(jnp.bfloat16))
        return pod_low.astype(jnp.float32)
    grad_low = lax.optimization_barrier(jnp.sum(lax.map(per_pod, (grad_values, grad_scales)), axis=0)).reshape(RANK, FFW)
    owned = grad_low[row_order]
    new_first = first_decay * first_moment + (1.0 - first_decay) * owned
    new_second = second_decay * second_moment + (1.0 - second_decay) * owned * owned
    corrected = new_first / (1.0 - first_decay ** step_count)
    spread = jnp.sqrt(new_second / (1.0 - second_decay ** step_count)) + 1e-08
    update = (corrected / spread).astype(jnp.bfloat16)
    direction = update[inverse]
    change = jnp.dot(projector, direction, preferred_element_type=jnp.float32)
    new_weights = (weights.astype(jnp.float32) - update_scale * change).astype(jnp.bfloat16)
    return (new_weights, new_first, new_second)
```

```python
import functools
import math

import jax
import jax.numpy as jnp
from jax import lax
from jax.experimental import pallas as pl
from jax.experimental.pallas import tpu as pltpu
from jax.sharding import PartitionSpec as P

first_decay = 0.9
second_decay = 0.999
step_count = 100.0
update_scale = 0.25


def bits_of(count):
    return range(count.bit_length() - 1)


def largest_divisor(count, limit):
    return max(d for d in range(1, limit + 1) if count % d == 0)


def swap(array, stage):
    axis, bit = stage
    size = lax.axis_size(axis)
    return lax.ppermute(array, axis, [(i, i ^ (1 << bit)) for i in range(size)])


def prepare_kernel(first_block, position_ref, values_ref, scales_ref, keep_ref, send_ref):
    rows, width = values_ref.shape
    blocks = scales_ref.shape[1]
    block_width = 128
    step_blocks = width // block_width
    placing = (
        lax.broadcasted_iota(jnp.int32, (rows, rows), 0) == position_ref[...]
    ).astype(jnp.bfloat16)
    block = lax.broadcasted_iota(jnp.int32, (blocks, width), 1) // block_width
    block = block + first_block + pl.program_id(0) * step_blocks
    spread = (block == lax.broadcasted_iota(jnp.int32, (blocks, width), 0)).astype(jnp.bfloat16)
    scales = jnp.dot(scales_ref[...], spread, preferred_element_type=jnp.float32)
    terms = (values_ref[...].astype(jnp.float32) * scales).astype(jnp.bfloat16)
    placed = jnp.dot(placing, terms, preferred_element_type=jnp.float32).astype(jnp.bfloat16)
    keep_ref[...] = placed[: rows // 2]
    send_ref[...] = placed[rows // 2 :]


def prepare(values, scales, position, start, count, block_width):
    rows = values.shape[0]
    step = largest_divisor(math.gcd(start, count), 8)
    assert block_width == 128
    half = jax.ShapeDtypeStruct((rows // 2, count * block_width), jnp.bfloat16)
    out = pl.BlockSpec((rows // 2, step * block_width), lambda i: (0, i))
    return pl.pallas_call(
        functools.partial(prepare_kernel, start),
        grid=(count // step,),
        in_specs=[
            pl.BlockSpec((1, rows), lambda i: (0, 0)),
            pl.BlockSpec((rows, step * block_width), lambda i: (0, start // step + i)),
            pl.BlockSpec(scales.shape, lambda i: (0, 0)),
        ],
        out_specs=[out, out],
        out_shape=[half, half],
        compiler_params=pltpu.CompilerParams(vmem_limit_bytes=48 * 1024 * 1024),
        cost_estimate=pl.CostEstimate(
            flops=2 * rows * rows * count * block_width,
            bytes_accessed=4 * rows * count * block_width,
            transcendentals=0,
        ),
        name="prepare",
    )(position, values, scales)


def apply_kernel(projector_ref, weights_ref, *refs):
    pieces, out_ref = refs[:4], refs[-1]
    direction = jnp.concatenate([piece[...] for piece in pieces], axis=0)
    change = jnp.dot(projector_ref[...], direction, preferred_element_type=jnp.float32)
    out_ref[...] = (weights_ref[...].astype(jnp.float32) - update_scale * change).astype(
        out_ref.dtype
    )


def apply_update(projector, weights, pieces, so_far, start, count, block_width):
    rows = weights.shape[0]
    rank = projector.shape[1]
    step = largest_divisor(math.gcd(start, count), 8)
    width = step * block_width
    aliased = [] if so_far is None else [so_far]
    return pl.pallas_call(
        apply_kernel,
        grid=(count // step,),
        in_specs=[
            pl.BlockSpec(projector.shape, lambda i: (0, 0)),
            pl.BlockSpec((rows, width), lambda i: (0, start // step + i)),
        ]
        + [pl.BlockSpec((piece.shape[0], width), lambda i: (0, i)) for piece in pieces]
        + [pl.BlockSpec(memory_space=pl.ANY) for _ in aliased],
        out_specs=pl.BlockSpec((rows, width), lambda i: (0, start // step + i)),
        out_shape=jax.ShapeDtypeStruct(weights.shape, weights.dtype),
        input_output_aliases={} if so_far is None else {2 + len(pieces): 0},
        compiler_params=pltpu.CompilerParams(vmem_limit_bytes=48 * 1024 * 1024),
        cost_estimate=pl.CostEstimate(
            flops=2 * rows * rank * count * block_width,
            bytes_accessed=6 * rows * count * block_width,
            transcendentals=0,
        ),
        name="apply_update",
    )(projector, weights, *pieces, *aliased)


def added(left, right):
    return (left.astype(jnp.float32) + right.astype(jnp.float32)).astype(jnp.bfloat16)


def per_device(
    grad_values, grad_scales, block_owner, projector, weights, first_moment, second_moment
):
    shards, outers = lax.axis_size("shard"), lax.axis_size("outer")
    shard, outer = lax.axis_index("shard"), lax.axis_index("outer")
    rank_rows = block_owner.shape[0]
    owned_rows = rank_rows // shards
    leaf_rows = owned_rows // outers
    values = grad_values[0, 0]
    scales = grad_scales[0, 0]
    col_blocks = scales.shape[1]
    block_width = values.shape[1] // col_blocks

    row_index = jnp.arange(rank_rows, dtype=jnp.int32)
    earlier = (block_owner[None, :] == block_owner[:, None]) & (
        row_index[None, :] < row_index[:, None]
    )
    rank_in_owner = jnp.sum(earlier.astype(jnp.int32), axis=1)
    away = {"shard": block_owner ^ shard, "outer": (rank_in_owner // leaf_rows) ^ outer}

    shard_stages = [("shard", bit) for bit in bits_of(shards)]
    outer_stages = [("outer", bit) for bit in bits_of(outers)]
    core, inner, last = shard_stages[0], shard_stages[1:-1], shard_stages[-1]
    turning = inner[:1] + outer_stages + inner[1:]
    orders = [turning[turn:] + turning[:turn] + [last] for turn in range(3)]
    unit = largest_divisor(col_blocks, 4)
    units = col_blocks // unit
    counts = [unit * ((units + 2 - turn) // 3) for turn in range(3)]
    starts = [sum(counts[:turn]) for turn in range(3)]

    placings, held = [], []
    for order, start, count in zip(orders, starts, counts):
        position = jnp.zeros_like(block_owner)
        for axis, bit in [core] + order:
            position = 2 * position + ((away[axis] >> bit) & 1)
        position = position * leaf_rows + rank_in_owner % leaf_rows
        placings.append((position[None, :] == row_index[:, None]).astype(jnp.bfloat16))
        held.append(prepare(values, scales, position[None, :], start, count, block_width))

    partial = []
    for keep, send in held:
        partial.append((keep, swap(send, core)))
    for step in range(len(orders[0])):
        for turn, order in enumerate(orders):
            mine, came = partial[turn]
            half = mine.shape[0] // 2
            send = added(mine[half:], came[half:])
            keep = added(mine[:half], came[:half])
            partial[turn] = (keep, swap(send, order[step]))
    owned_parts = [added(mine, came) for mine, came in partial]

    def normalized(owned, first, second):
        new_first = first_decay * first + (1.0 - first_decay) * owned
        new_second = second_decay * second + (1.0 - second_decay) * owned * owned
        return new_first, new_second

    gathered = []
    for owned, start, count in zip(owned_parts, starts, counts):
        own = (outer * leaf_rows, start * block_width)
        shape = (leaf_rows, count * block_width)
        new_first, new_second = normalized(
            owned.astype(jnp.float32),
            lax.dynamic_slice(first_moment, own, shape),
            lax.dynamic_slice(second_moment, own, shape),
        )
        corrected = new_first / (1.0 - first_decay**step_count)
        spread = jnp.sqrt(new_second / (1.0 - second_decay**step_count)) + 1e-08
        gathered.append((corrected / spread).astype(jnp.bfloat16))
    steps = len(orders[0])
    for step in reversed(range(1, steps)):
        for turn, order in enumerate(orders):
            mine = gathered[turn]
            gathered[turn] = jnp.concatenate([mine, swap(mine, order[step])], axis=0)
    pieces = []
    for mine, order in zip(gathered, orders):
        pieces.append((mine, swap(mine, order[0]), swap(mine, core)))

    owned = jnp.concatenate(owned_parts, axis=1)
    for stage in outer_stages:
        other = swap(owned, stage)
        low = ((outer >> stage[1]) & 1) == 0
        owned = jnp.where(
            low,
            jnp.concatenate([owned, other], axis=0),
            jnp.concatenate([other, owned], axis=0),
        )
    new_first, new_second = normalized(owned.astype(jnp.float32), first_moment, second_moment)

    new_weights = None
    for turn in range(3):
        mine, came, beside = pieces[turn]
        reordered = jnp.dot(
            projector, placings[turn].T, preferred_element_type=jnp.float32
        ).astype(jnp.bfloat16)
        new_weights = apply_update(
            reordered,
            weights,
            (mine, came, beside, swap(came, core)),
            new_weights,
            starts[turn],
            counts[turn],
            block_width,
        )
    return (new_weights, new_first, new_second)


def solution(mesh):
    placed = (
        P("outer", "shard", None, None),
        P("outer", "shard", None, None),
        P(),
        P(("outer", "shard"), None),
        P(("outer", "shard"), None),
        P("shard", None),
        P("shard", None),
    )
    return jax.shard_map(
        per_device,
        mesh=mesh,
        in_specs=placed,
        out_specs=(P(("outer", "shard"), None), P("shard", None), P("shard", None)),
        check_vma=False,
    )
```

```python
import functools

import jax
import jax.numpy as jnp
from jax import lax
from jax.experimental import pallas as pl
from jax.experimental.pallas import tpu as pltpu
from jax.sharding import PartitionSpec as P

first_decay = 0.9
second_decay = 0.999
step_count = 100.0
update_scale = 0.25
both = ("outer", "shard")
chains = ((1, 0, 1), (1, 2, 0), (1, 1, 2), (1, 0, 1))


def bits_of(count):
    return list(range(count.bit_length() - 1))


def largest_divisor(count, limit):
    return max(d for d in range(1, limit + 1) if count % d == 0)


def swap(array, bits):
    size = lax.axis_size("outer") * lax.axis_size("shard")
    return lax.ppermute(array, both, [(i, i ^ (1 << bits[i % 2])) for i in range(size)])


def axis_orders():
    shard_bits = bits_of(lax.axis_size("shard"))
    outer_bits = [len(shard_bits) + bit for bit in bits_of(lax.axis_size("outer"))]
    turning = shard_bits[1:2] + outer_bits + shard_bits[2:-1]
    return [turning[t:] + turning[:t] + shard_bits[-1:] for t in range(3)]


def prepare_kernel(
    first_block,
    block_width,
    orders,
    shards,
    leaf_rows,
    me_ref,
    owner_hbm,
    scales_hbm,
    values_ref,
    keep_ref,
    send_ref,
    placing_out_ref,
    owner_ref,
    scales_ref,
    wide_scales_ref,
    placing_ref,
    semaphores,
):
    rows, width = values_ref.shape
    step_blocks = width // block_width

    @pl.when(pl.program_id(0) == 0)
    def _():
        copies = [
            pltpu.make_async_copy(owner_hbm, owner_ref, semaphores.at[0]),
            pltpu.make_async_copy(scales_hbm, scales_ref, semaphores.at[1]),
        ]
        for copy in copies:
            copy.start()
        copies[0].wait()
        down = lax.broadcasted_iota(jnp.int32, (rows, rows), 0)
        across = lax.broadcasted_iota(jnp.int32, (rows, rows), 1)
        owner = owner_ref[...]
        owner_across = jnp.broadcast_to(owner, (rows, rows))
        earlier = (owner_across == owner_across.T) & (down < across)
        rank = jnp.sum(earlier.astype(jnp.int32), axis=0, keepdims=True)
        me = me_ref[0]
        away = ((rank // leaf_rows) * shards + owner) ^ me
        position = away & 1
        for bits in zip(*orders):
            bit = jnp.where(owner % 2 == 0, bits[0], bits[1])
            position = 2 * position + ((away >> bit) & 1)
        position = position * leaf_rows + rank % leaf_rows
        placing = (down == position).astype(jnp.bfloat16)
        placing_ref[...] = placing
        placing_out_ref[...] = placing
        copies[1].wait()
        wide_scales_ref[...] = scales_ref[...].astype(jnp.float32)

    placing = placing_ref[...]
    first = first_block + pl.program_id(0) * step_blocks
    for part in range(step_blocks):
        columns = slice(part * block_width, (part + 1) * block_width)
        scaled = placing * wide_scales_ref[pl.ds(first + part, 1), :].astype(jnp.bfloat16)
        placed = jnp.dot(
            scaled, values_ref[:, columns], preferred_element_type=jnp.float32
        ).astype(jnp.bfloat16)
        keep_ref[:, columns] = placed[: rows // 2]
        send_ref[:, columns] = placed[rows // 2 :]


def step_blocks(count):
    return largest_divisor(count, 30)


def columns_from(rows, width, first):
    return pl.BlockSpec(
        (pl.Element(rows), pl.Element(width)),
        lambda i, *_: (0, pl.multiple_of(first + i * width, 128)),
    )


def prepare(me, owner, values, scales, orders, start, count, shards, leaf_rows):
    rows = values.shape[0]
    block_width = values.shape[1] // scales.shape[0]
    step = step_blocks(count)
    width = step * block_width
    half = jax.ShapeDtypeStruct((rows // 2, count * block_width), jnp.bfloat16)
    out = pl.BlockSpec((rows // 2, width), lambda i, me: (0, i))
    return pl.pallas_call(
        functools.partial(prepare_kernel, start, block_width, orders, shards, leaf_rows),
        grid_spec=pltpu.PrefetchScalarGridSpec(
            num_scalar_prefetch=1,
            grid=(count // step,),
            in_specs=[
                pl.BlockSpec(memory_space=pltpu.HBM),
                pl.BlockSpec(memory_space=pltpu.HBM),
                columns_from(rows, width, start * block_width),
            ],
            out_specs=[out, out, pl.BlockSpec((rows, rows), lambda i, me: (0, 0))],
            scratch_shapes=[
                pltpu.VMEM(owner.shape, jnp.int32),
                pltpu.VMEM(scales.shape, scales.dtype),
                pltpu.VMEM(scales.shape, jnp.float32),
                pltpu.VMEM((rows, rows), jnp.bfloat16),
                pltpu.SemaphoreType.DMA((2,)),
            ],
        ),
        out_shape=[half, half, jax.ShapeDtypeStruct((rows, rows), jnp.bfloat16)],
        compiler_params=pltpu.CompilerParams(vmem_limit_bytes=20 * 1024 * 1024),
        cost_estimate=pl.CostEstimate(flops=1024, bytes_accessed=1024, transcendentals=0),
        name="prepare",
    )(me, owner, scales, values)


def apply_kernel(sub_width, projector_ref, placing_ref, weights_ref, *refs):
    pieces, out_ref, reordered_ref = refs[:4], refs[-2], refs[-1]

    @pl.when(pl.program_id(0) == 0)
    def _():
        reordered_ref[...] = lax.dot_general(
            projector_ref[...],
            placing_ref[...],
            (((1,), (1,)), ((), ())),
            preferred_element_type=jnp.float32,
        ).astype(jnp.bfloat16)

    for part in range(weights_ref.shape[1] // sub_width):
        columns = slice(part * sub_width, (part + 1) * sub_width)
        direction = jnp.concatenate([piece[:, columns] for piece in pieces], axis=0)
        change = jnp.dot(reordered_ref[...], direction, preferred_element_type=jnp.float32)
        out_ref[:, columns] = (
            weights_ref[:, columns].astype(jnp.float32) - update_scale * change
        ).astype(out_ref.dtype)


def apply_update(projector, placing, weights, pieces, so_far, start, count, block_width):
    rows = weights.shape[0]
    step = step_blocks(count)
    width = step * block_width
    sub_width = block_width * largest_divisor(step, 2)
    aliased = [] if so_far is None else [so_far]
    return pl.pallas_call(
        functools.partial(apply_kernel, sub_width),
        grid=(count // step,),
        in_specs=[
            pl.BlockSpec(projector.shape, lambda i: (0, 0)),
            pl.BlockSpec(placing.shape, lambda i: (0, 0)),
            columns_from(rows, width, start * block_width),
        ]
        + [pl.BlockSpec((piece.shape[0], width), lambda i: (0, i)) for piece in pieces]
        + [pl.BlockSpec(memory_space=pl.ANY) for _ in aliased],
        out_specs=columns_from(rows, width, start * block_width),
        out_shape=jax.ShapeDtypeStruct(weights.shape, weights.dtype),
        scratch_shapes=[pltpu.VMEM(projector.shape, jnp.bfloat16)],
        input_output_aliases={} if so_far is None else {3 + len(pieces): 0},
        compiler_params=pltpu.CompilerParams(vmem_limit_bytes=20 * 1024 * 1024),
        cost_estimate=pl.CostEstimate(flops=1024, bytes_accessed=1024, transcendentals=0),
        name="apply_update",
    )(projector, placing, weights, *pieces, *aliased)


def added(left, right):
    return (left.astype(jnp.float32) + right.astype(jnp.float32)).astype(jnp.bfloat16)


def normalized(owned, first, second):
    new_first = first_decay * first + (1.0 - first_decay) * owned
    new_second = second_decay * second + (1.0 - second_decay) * owned * owned
    return new_first, new_second


def per_device(
    grad_values, grad_scales, block_owner, projector, weights, first_moment, second_moment
):
    shards, outers = lax.axis_size("shard"), lax.axis_size("outer")
    outer = lax.axis_index("outer")
    rank_rows = block_owner.shape[0]
    leaf_rows = rank_rows // shards // outers
    values = grad_values[0, 0]
    scales = grad_scales[0, 0].T
    col_blocks = scales.shape[0]
    block_width = values.shape[1] // col_blocks
    me = lax.axis_index(both).astype(jnp.int32)[None]

    turns = axis_orders()
    stages = len(turns[0])
    unit = largest_divisor(col_blocks, 4)
    units = col_blocks // unit
    total = sum(share for share, _, _ in chains)
    ends = [
        unit * round(units * sum(share for share, _, _ in chains[: i + 1]) / total)
        for i in range(len(chains))
    ]
    starts = [0] + ends[:-1]
    counts = [end - start for start, end in zip(starts, ends)]
    orders = [(turns[left], turns[right]) for _, left, right in chains]
    every = range(len(chains))

    last = [me]

    def turn_of(*arrays):
        return lax.optimization_barrier((*arrays, last[0]))[:-1]

    bits = [list(zip(*order)) for order in orders]
    partial, placing, gathered, owned_parts = {}, {}, {}, {}

    def prepare_chain(i):
        (turned_owner,) = turn_of(block_owner)
        keep, send, placing[i] = prepare(
            me,
            turned_owner[None, :],
            values,
            scales,
            orders[i],
            starts[i],
            counts[i],
            shards,
            leaf_rows,
        )
        partial[i] = (keep, swap(send, (0, 0)))
        last[0] = send

    def reduce_stage(i, stage):
        mine, came = turn_of(*partial[i])
        half = mine.shape[0] // 2
        send = added(mine[half:], came[half:])
        partial[i] = (None, swap(send, bits[i][stage]))
        mine, came, _ = lax.optimization_barrier((mine, came, send))
        keep = added(mine[:half], came[:half])
        partial[i] = (keep, partial[i][1])
        last[0] = send

    def update_stage(i):
        mine, came = turn_of(*partial[i])
        owned_parts[i] = added(mine, came)
        own = (outer * leaf_rows, starts[i] * block_width)
        shape = (leaf_rows, counts[i] * block_width)
        new_first, new_second = normalized(
            owned_parts[i].astype(jnp.float32),
            lax.dynamic_slice(first_moment, own, shape),
            lax.dynamic_slice(second_moment, own, shape),
        )
        corrected = new_first / (1.0 - first_decay**step_count)
        spread = jnp.sqrt(new_second / (1.0 - second_decay**step_count)) + 1e-08
        update = (corrected / spread).astype(jnp.bfloat16)
        gathered[i] = (update, swap(update, bits[i][-1]))
        last[0] = update

    def gather_stage(i, stage):
        mine = jnp.concatenate(turn_of(*gathered[i]), axis=0)
        gathered[i] = (mine, swap(mine, bits[i][stage]))
        last[0] = mine

    def owned_by_shard():
        owned = jnp.concatenate([owned_parts[i] for i in every], axis=1)
        for bit in bits_of(outers):
            other = swap(owned, (len(bits_of(shards)) + bit,) * 2)
            low = ((outer >> bit) & 1) == 0
            owned = jnp.where(
                low,
                jnp.concatenate([owned, other], axis=0),
                jnp.concatenate([other, owned], axis=0),
            )
        return owned

    def moments(owned):
        (owned,) = turn_of(owned)
        moved = normalized(owned.astype(jnp.float32), first_moment, second_moment)
        last[0] = moved[0]
        return moved

    for i in every:
        prepare_chain(i)
    for stage in range(stages):
        for i in every:
            reduce_stage(i, stage)
    for i in every:
        update_stage(i)
    owned = owned_by_shard()
    for stage in reversed(range(stages - 1)):
        if stage == 0:
            new_first, new_second = moments(owned)
        for i in every:
            gather_stage(i, stage)
    new_weights = None
    forwarded = {}
    for i in every:
        mine, came = gathered[i]
        beside = swap(mine, (0, 0))
        (came,) = turn_of(came)
        forwarded[i] = (mine, came, beside, swap(came, (0, 0)))
        last[0] = came
    for i in every:
        new_weights = apply_update(
            projector,
            placing[i],
            weights,
            turn_of(*forwarded[i]),
            new_weights,
            starts[i],
            counts[i],
            block_width,
        )
        last[0] = new_weights
    return (new_weights, new_first, new_second)


def solution(mesh):
    placed = (
        P("outer", "shard", None, None),
        P("outer", "shard", None, None),
        P(),
        P(("outer", "shard"), None),
        P(("outer", "shard"), None),
        P("shard", None),
        P("shard", None),
    )
    return jax.shard_map(
        per_device,
        mesh=mesh,
        in_specs=placed,
        out_specs=(P(("outer", "shard"), None), P("shard", None), P("shard", None)),
        check_vma=False,
    )
```

```python
import functools

import jax
import jax.numpy as jnp
from jax import lax
from jax.experimental import pallas as pl
from jax.experimental.pallas import tpu as pltpu
from jax.sharding import PartitionSpec as P

first_decay = 0.9
second_decay = 0.999
step_count = 100.0
update_scale = 0.25
both = ("outer", "shard")
chains = ((1, 0, 1), (1, 2, 0), (1, 1, 2), (1, 0, 1))


runs_per_chain = 2
slots = 3
lags = (0, 0, 0, 0)


def bits_of(count):
    return list(range(count.bit_length() - 1))


def swap(array, bits):
    size = lax.axis_size("outer") * lax.axis_size("shard")
    return lax.ppermute(array, both, [(i, i ^ (1 << bits[i % 2])) for i in range(size)])


def axis_orders():
    shard_bits = bits_of(lax.axis_size("shard"))
    outer_bits = [len(shard_bits) + bit for bit in bits_of(lax.axis_size("outer"))]
    turning = shard_bits[1:2] + outer_bits + shard_bits[2:-1]
    return [turning[t:] + turning[:t] + shard_bits[-1:] for t in range(3)]


def pieces_of(start, count):
    ends = [start + count * (run + 1) // runs_per_chain for run in range(runs_per_chain)]
    return [(at, end - at) for at, end in zip([start] + ends, ends) if end > at]


def prepare_kernel(spans, block_width, orders, shards, leaf_rows, me_ref, *refs):
    chain_count = len(spans)
    owner_hbm, scales_hbm, values_hbm = refs[:3]
    keep_refs, send_refs = refs[3 : 3 + chain_count], refs[3 + chain_count : 3 + 2 * chain_count]
    position_ref, owner_ref, scales_ref, wide_scales_ref, in_ref, keep_ref, send_ref = refs[
        3 + 2 * chain_count : -3
    ]
    small_sems, in_sems, out_sems = refs[-3:]
    rows = in_ref.shape[1]
    half = rows // 2
    runs = [
        (chain, at, size)
        for chain, (start, count) in enumerate(spans)
        for at, size in pieces_of(start, count)
    ]

    def incoming(index):
        _, at, size = runs[index]
        slot = index % slots
        return pltpu.make_async_copy(
            values_hbm.at[:, pl.ds(at * block_width, size * block_width)],
            in_ref.at[slot, :, pl.ds(0, size * block_width)],
            in_sems.at[slot],
        )

    def outgoing(index):
        chain, at, size = runs[index]
        slot = index % slots
        columns = pl.ds(0, size * block_width)
        target = pl.ds((at - spans[chain][0]) * block_width, size * block_width)
        return [
            pltpu.make_async_copy(
                buffer.at[slot, :, columns], outs[chain].at[:, target], out_sems.at[slot, which]
            )
            for which, (buffer, outs) in enumerate(((keep_ref, keep_refs), (send_ref, send_refs)))
        ]

    owner_copy = pltpu.make_async_copy(owner_hbm, owner_ref, small_sems.at[0])
    scales_copy = pltpu.make_async_copy(scales_hbm, scales_ref, small_sems.at[1])
    owner_copy.start()
    scales_copy.start()
    for index in range(min(slots - 1, len(runs))):
        incoming(index).start()
    owner_copy.wait()
    down = lax.broadcasted_iota(jnp.int32, (rows, rows), 0)
    across = lax.broadcasted_iota(jnp.int32, (rows, rows), 1)
    owner = owner_ref[...]
    owner_across = jnp.broadcast_to(owner, (rows, rows))
    earlier = (owner_across == owner_across.T) & (down < across)
    rank = jnp.sum(earlier.astype(jnp.int32), axis=0, keepdims=True)
    away = ((rank // leaf_rows) * shards + owner) ^ me_ref[0]
    for chain in range(chain_count):
        position = away & 1
        for bits in zip(*orders[chain]):
            bit = jnp.where(owner % 2 == 0, bits[0], bits[1])
            position = 2 * position + ((away >> bit) & 1)
        position_ref[chain] = position * leaf_rows + rank % leaf_rows
    scales_copy.wait()
    wide_scales_ref[...] = scales_ref[...].astype(jnp.float32)

    for index, (chain, at, size) in enumerate(runs):
        slot = index % slots
        if index + slots - 1 < len(runs):
            incoming(index + slots - 1).start()
        incoming(index).wait()
        if index >= slots:
            for copy in outgoing(index - slots):
                copy.wait()
        placing = (down == position_ref[chain]).astype(jnp.bfloat16)
        for block in range(size):
            columns = slice(block * block_width, (block + 1) * block_width)
            scale = wide_scales_ref[at + block : at + block + 1, :].astype(jnp.bfloat16)
            placed = jnp.dot(
                placing * scale, in_ref[slot, :, columns], preferred_element_type=jnp.float32
            ).astype(jnp.bfloat16)
            keep_ref[slot, :, columns] = placed[:half]
            send_ref[slot, :, columns] = placed[half:]
        for copy in outgoing(index):
            copy.start()
    for index in range(max(0, len(runs) - slots), len(runs)):
        for copy in outgoing(index):
            copy.wait()


def prepare(me, owner, values, scales, orders, spans, shards, leaf_rows):
    rows = values.shape[0]
    block_width = values.shape[1] // scales.shape[0]
    longest = max(size for span in spans for _, size in pieces_of(*span)) * block_width
    halves = [
        jax.ShapeDtypeStruct((rows // 2, count * block_width), jnp.bfloat16) for _, count in spans
    ]
    anywhere = pl.BlockSpec(memory_space=pl.ANY)
    *parts, position = pl.pallas_call(
        functools.partial(prepare_kernel, spans, block_width, orders, shards, leaf_rows),
        in_specs=[pl.BlockSpec(memory_space=pltpu.SMEM)] + [anywhere] * 3,
        out_specs=[anywhere] * (2 * len(spans)) + [pl.BlockSpec(memory_space=pltpu.VMEM)],
        out_shape=halves * 2 + [jax.ShapeDtypeStruct((len(spans), 1, rows), jnp.int32)],
        scratch_shapes=[
            pltpu.VMEM(owner.shape, jnp.int32),
            pltpu.VMEM(scales.shape, scales.dtype),
            pltpu.VMEM(scales.shape, jnp.float32),
            pltpu.VMEM((slots, rows, longest), jnp.bfloat16),
            pltpu.VMEM((slots, rows // 2, longest), jnp.bfloat16),
            pltpu.VMEM((slots, rows // 2, longest), jnp.bfloat16),
            pltpu.SemaphoreType.DMA((2,)),
            pltpu.SemaphoreType.DMA((slots,)),
            pltpu.SemaphoreType.DMA((slots, 2)),
        ],
        compiler_params=pltpu.CompilerParams(vmem_limit_bytes=56 * 1024 * 1024),
        cost_estimate=pl.CostEstimate(flops=1024, bytes_accessed=1024, transcendentals=0),
        name="prepare",
    )(me, owner, scales, values)
    return parts[: len(spans)], parts[len(spans) :], position


def apply_kernel(chosen, spans, block_width, projector_ref, position_ref, weights_hbm, *refs):
    chain_count = len(spans)
    pieces = refs[: 4 * chain_count]
    out_hbm, reordered_ref, weights_ref, direction_ref, out_ref, in_sems, out_sems = refs[-7:]
    rank = projector_ref.shape[1]
    quarter = rank // 4
    runs = [
        (chain, at, size)
        for chain, (start, count) in enumerate(spans)
        for at, size in pieces_of(start, count)
    ]

    def incoming(index):
        chain, at, size = runs[index]
        slot = index % slots
        columns = pl.ds(0, size * block_width)
        source = pl.ds((at - spans[chain][0]) * block_width, size * block_width)
        return [
            pltpu.make_async_copy(
                weights_hbm.at[:, pl.ds(at * block_width, size * block_width)],
                weights_ref.at[slot, :, columns],
                in_sems.at[slot, 4],
            )
        ] + [
            pltpu.make_async_copy(
                pieces[4 * chain + part].at[:, source],
                direction_ref.at[slot, pl.ds(part * quarter, quarter), columns],
                in_sems.at[slot, part],
            )
            for part in range(4)
        ]

    def outgoing(index):
        _, at, size = runs[index]
        slot = index % slots
        return pltpu.make_async_copy(
            out_ref.at[slot, :, pl.ds(0, size * block_width)],
            out_hbm.at[:, pl.ds(at * block_width, size * block_width)],
            out_sems.at[slot],
        )

    for index in range(min(slots - 1, len(runs))):
        for copy in incoming(index):
            copy.start()
    down = lax.broadcasted_iota(jnp.int32, (rank, rank), 0)
    for chain in range(chain_count):
        placing = (down == position_ref[chosen[chain]]).astype(jnp.bfloat16)
        reordered_ref[chain] = lax.dot_general(
            projector_ref[...],
            placing,
            (((1,), (1,)), ((), ())),
            preferred_element_type=jnp.float32,
        ).astype(jnp.bfloat16)
    for index, (chain, at, size) in enumerate(runs):
        slot = index % slots
        if index + slots - 1 < len(runs):
            for copy in incoming(index + slots - 1):
                copy.start()
        for copy in incoming(index):
            copy.wait()
        if index >= slots:
            outgoing(index - slots).wait()
        for block in range(0, size, 2):
            columns = slice(block * block_width, min(block + 2, size) * block_width)
            change = jnp.dot(
                reordered_ref[chain],
                direction_ref[slot, :, columns],
                preferred_element_type=jnp.float32,
            )
            out_ref[slot, :, columns] = (
                weights_ref[slot, :, columns].astype(jnp.float32) - update_scale * change
            ).astype(out_ref.dtype)
        outgoing(index).start()
    for index in range(max(0, len(runs) - slots), len(runs)):
        outgoing(index).wait()


def apply_update(projector, position, weights, pieces, so_far, chosen, spans, block_width):
    rows, rank = projector.shape
    longest = max(size for span in spans for _, size in pieces_of(*span)) * block_width
    whole = pl.BlockSpec(memory_space=pltpu.VMEM)
    anywhere = pl.BlockSpec(memory_space=pl.ANY)
    aliased = [] if so_far is None else [so_far]
    return pl.pallas_call(
        functools.partial(apply_kernel, chosen, spans, block_width),
        in_specs=[whole, whole] + [anywhere] * (1 + len(pieces) + len(aliased)),
        out_specs=anywhere,
        input_output_aliases={3 + len(pieces): 0} if aliased else {},
        out_shape=jax.ShapeDtypeStruct(weights.shape, weights.dtype),
        scratch_shapes=[
            pltpu.VMEM((len(spans), rows, rank), jnp.bfloat16),
            pltpu.VMEM((slots, rows, longest), jnp.bfloat16),
            pltpu.VMEM((slots, rank, longest), jnp.bfloat16),
            pltpu.VMEM((slots, rows, longest), jnp.bfloat16),
            pltpu.SemaphoreType.DMA((slots, 5)),
            pltpu.SemaphoreType.DMA((slots,)),
        ],
        compiler_params=pltpu.CompilerParams(vmem_limit_bytes=20 * 1024 * 1024),
        cost_estimate=pl.CostEstimate(flops=1024, bytes_accessed=1024, transcendentals=0),
        name="apply_update",
    )(projector, position, weights, *pieces, *aliased)


def added(terms):
    return sum(term.astype(jnp.float32) for term in terms).astype(jnp.bfloat16)


def normalized(owned, first, second):
    new_first = first_decay * first + (1.0 - first_decay) * owned
    new_second = second_decay * second + (1.0 - second_decay) * owned * owned
    return new_first, new_second


def per_device(
    grad_values, grad_scales, block_owner, projector, weights, first_moment, second_moment
):
    shards, outers = lax.axis_size("shard"), lax.axis_size("outer")
    outer = lax.axis_index("outer")
    rank_rows = block_owner.shape[0]
    leaf_rows = rank_rows // shards // outers
    values = grad_values[0, 0]
    scales = grad_scales[0, 0].T
    col_blocks = scales.shape[0]
    block_width = values.shape[1] // col_blocks
    me = lax.axis_index(both).astype(jnp.int32)[None]

    turns = axis_orders()
    stages = len(turns[0])
    total = sum(share for share, _, _ in chains)
    ends = [
        round(col_blocks * sum(share for share, _, _ in chains[: i + 1]) / total)
        for i in range(len(chains))
    ]
    starts = [0] + ends[:-1]
    counts = [end - start for start, end in zip(starts, ends)]
    spans = list(zip(starts, counts))
    orders = [(turns[left], turns[right]) for _, left, right in chains]
    every = range(len(chains))

    last = [me]

    def turn_of(*arrays):
        return lax.optimization_barrier((*arrays, last[0]))[:-1]

    bits = [list(zip(*order)) for order in orders]
    partial, gathered, owned_parts = {}, {}, {}

    def reduce_stage(i, stage):
        mine, came = turn_of(*partial[i])
        half = mine.shape[0] // 2
        send = added([mine[half:], came[half:]])
        sent = swap(send, bits[i][stage])
        mine, came, last[0] = lax.optimization_barrier((mine, came, send))
        partial[i] = (added([mine[:half], came[:half]]), sent)

    def update_stage(i):
        owned_parts[i] = added(turn_of(*partial[i]))
        own = (outer * leaf_rows, starts[i] * block_width)
        shape = (leaf_rows, counts[i] * block_width)
        new_first, new_second = normalized(
            owned_parts[i].astype(jnp.float32),
            lax.dynamic_slice(first_moment, own, shape),
            lax.dynamic_slice(second_moment, own, shape),
        )
        corrected = new_first / (1.0 - first_decay**step_count)
        spread = jnp.sqrt(new_second / (1.0 - second_decay**step_count)) + 1e-08
        update = (corrected / spread).astype(jnp.bfloat16)
        gathered[i] = (update, swap(update, bits[i][-1]))
        last[0] = update

    def gather_stage(i, stage):
        mine = jnp.concatenate(turn_of(*gathered[i]), axis=0)
        gathered[i] = (mine, swap(mine, bits[i][stage]))
        last[0] = mine

    def owned_by_shard():
        owned = jnp.concatenate([owned_parts[i] for i in every], axis=1)
        for bit in bits_of(outers):
            other = swap(owned, (len(bits_of(shards)) + bit,) * 2)
            low = ((outer >> bit) & 1) == 0
            owned = jnp.where(
                low,
                jnp.concatenate([owned, other], axis=0),
                jnp.concatenate([other, owned], axis=0),
            )
        return owned

    def moments(owned):
        (owned,) = turn_of(owned)
        moved = normalized(owned.astype(jnp.float32), first_moment, second_moment)
        last[0] = moved[0]
        return moved

    keeps, sends, position = prepare(
        me, block_owner[None, :], values, scales, orders, spans, shards, leaf_rows
    )
    for i in every:
        partial[i] = [keeps[i], swap(sends[i], (0, 0))]
    owned = new_first = new_second = None
    work = [(stage + lags[i], i, stage) for i in every for stage in range(2 * stages)]
    for _, i, stage in sorted(work):
        if stage < stages:
            reduce_stage(i, stage)
        elif stage == stages:
            update_stage(i)
            if len(owned_parts) == len(chains):
                owned = owned_by_shard()
        else:
            if stage == 2 * stages - 1 and new_first is None:
                new_first, new_second = moments(owned)
            gather_stage(i, 2 * stages - 1 - stage)
    forwarded = {}
    for i in every:
        mine, came = gathered[i]
        beside = swap(mine, (0, 0))
        (came,) = turn_of(came)
        forwarded[i] = (mine, came, beside, swap(came, (0, 0)))
        last[0] = came
    new_weights = None
    for chosen in ((0, 1), (2, 3)):
        new_weights = last[0] = apply_update(
            projector,
            position,
            weights,
            turn_of(*[piece for i in chosen for piece in forwarded[i]]),
            new_weights,
            chosen,
            [spans[i] for i in chosen],
            block_width,
        )
    return (new_weights, new_first, new_second)


def solution(mesh):
    placed = (
        P("outer", "shard", None, None),
        P("outer", "shard", None, None),
        P(),
        P(("outer", "shard"), None),
        P(("outer", "shard"), None),
        P("shard", None),
        P("shard", None),
    )
    return jax.shard_map(
        per_device,
        mesh=mesh,
        in_specs=placed,
        out_specs=(P(("outer", "shard"), None), P("shard", None), P("shard", None)),
        check_vma=False,
    )
```

```python
import functools

import jax
import jax.numpy as jnp
from jax import lax
from jax.experimental import pallas as pl
from jax.experimental.pallas import tpu as pltpu
from jax.sharding import PartitionSpec as P

first_decay = 0.9
second_decay = 0.999
step_count = 100.0
update_scale = 0.25
both = ("outer", "shard")
chains = ((1, 0, 1), (1, 2, 0), (1, 1, 2), (1, 0, 1))


runs_per_chain = 2
slots = 3
lags = (0, 0, 0, 0)


def bits_of(count):
    return list(range(count.bit_length() - 1))


def swap(array, bits):
    size = lax.axis_size("outer") * lax.axis_size("shard")
    return lax.ppermute(array, both, [(i, i ^ (1 << bits[i % 2])) for i in range(size)])


def axis_orders():
    shard_bits = bits_of(lax.axis_size("shard"))
    outer_bits = [len(shard_bits) + bit for bit in bits_of(lax.axis_size("outer"))]
    turning = shard_bits[1:2] + outer_bits + shard_bits[2:-1]
    return [turning[t:] + turning[:t] + shard_bits[-1:] for t in range(3)]


def pieces_of(start, count):
    ends = [start + count * (run + 1) // runs_per_chain for run in range(runs_per_chain)]
    return [(at, end - at) for at, end in zip([start] + ends, ends) if end > at]


def prepare_kernel(spans, block_width, orders, shards, leaf_rows, me_ref, *refs):
    chain_count = len(spans)
    owner_hbm, scales_hbm, values_hbm = refs[:3]
    keep_refs, send_refs = refs[3 : 3 + chain_count], refs[3 + chain_count : 3 + 2 * chain_count]
    position_ref, owner_ref, scales_ref, wide_scales_ref, in_ref, keep_ref, send_ref = refs[
        3 + 2 * chain_count : -3
    ]
    small_sems, in_sems, out_sems = refs[-3:]
    rows = in_ref.shape[1]
    half = rows // 2
    runs = [
        (chain, at, size)
        for chain, (start, count) in enumerate(spans)
        for at, size in pieces_of(start, count)
    ]

    def incoming(index):
        _, at, size = runs[index]
        slot = index % slots
        return pltpu.make_async_copy(
            values_hbm.at[:, pl.ds(at * block_width, size * block_width)],
            in_ref.at[slot, :, pl.ds(0, size * block_width)],
            in_sems.at[slot],
        )

    def outgoing(index):
        chain, at, size = runs[index]
        slot = index % slots
        columns = pl.ds(0, size * block_width)
        target = pl.ds((at - spans[chain][0]) * block_width, size * block_width)
        return [
            pltpu.make_async_copy(
                buffer.at[slot, :, columns], outs[chain].at[:, target], out_sems.at[slot, which]
            )
            for which, (buffer, outs) in enumerate(((keep_ref, keep_refs), (send_ref, send_refs)))
        ]

    owner_copy = pltpu.make_async_copy(owner_hbm, owner_ref, small_sems.at[0])
    scales_copy = pltpu.make_async_copy(scales_hbm, scales_ref, small_sems.at[1])
    owner_copy.start()
    scales_copy.start()
    for index in range(min(slots - 1, len(runs))):
        incoming(index).start()
    owner_copy.wait()
    down = lax.broadcasted_iota(jnp.int32, (rows, rows), 0)
    across = lax.broadcasted_iota(jnp.int32, (rows, rows), 1)
    owner = owner_ref[...]
    owner_across = jnp.broadcast_to(owner, (rows, rows))
    earlier = (owner_across == owner_across.T) & (down < across)
    rank = jnp.sum(earlier.astype(jnp.int32), axis=0, keepdims=True)
    away = ((rank // leaf_rows) * shards + owner) ^ me_ref[0]
    for chain in range(chain_count):
        position = away & 1
        for bits in zip(*orders[chain]):
            bit = jnp.where(owner % 2 == 0, bits[0], bits[1])
            position = 2 * position + ((away >> bit) & 1)
        position_ref[chain] = position * leaf_rows + rank % leaf_rows
    scales_copy.wait()
    wide_scales_ref[...] = scales_ref[...].astype(jnp.float32)

    for index, (chain, at, size) in enumerate(runs):
        slot = index % slots
        if index + slots - 1 < len(runs):
            incoming(index + slots - 1).start()
        incoming(index).wait()
        if index >= slots:
            for copy in outgoing(index - slots):
                copy.wait()
        placing = (down == position_ref[chain]).astype(jnp.bfloat16)
        for block in range(size):
            columns = slice(block * block_width, (block + 1) * block_width)
            scale = wide_scales_ref[at + block : at + block + 1, :].astype(jnp.bfloat16)
            placed = jnp.dot(
                placing * scale, in_ref[slot, :, columns], preferred_element_type=jnp.float32
            ).astype(jnp.bfloat16)
            keep_ref[slot, :, columns] = placed[:half]
            send_ref[slot, :, columns] = placed[half:]
        for copy in outgoing(index):
            copy.start()
    for index in range(max(0, len(runs) - slots), len(runs)):
        for copy in outgoing(index):
            copy.wait()


def prepare(me, owner, values, scales, orders, spans, shards, leaf_rows):
    rows = values.shape[0]
    block_width = values.shape[1] // scales.shape[0]
    longest = max(size for span in spans for _, size in pieces_of(*span)) * block_width
    halves = [
        jax.ShapeDtypeStruct((rows // 2, count * block_width), jnp.bfloat16) for _, count in spans
    ]
    anywhere = pl.BlockSpec(memory_space=pl.ANY)
    *parts, position = pl.pallas_call(
        functools.partial(prepare_kernel, spans, block_width, orders, shards, leaf_rows),
        in_specs=[pl.BlockSpec(memory_space=pltpu.SMEM)] + [anywhere] * 3,
        out_specs=[anywhere] * (2 * len(spans)) + [pl.BlockSpec(memory_space=pltpu.VMEM)],
        out_shape=halves * 2 + [jax.ShapeDtypeStruct((len(spans), 1, rows), jnp.int32)],
        scratch_shapes=[
            pltpu.VMEM(owner.shape, jnp.int32),
            pltpu.VMEM(scales.shape, scales.dtype),
            pltpu.VMEM(scales.shape, jnp.float32),
            pltpu.VMEM((slots, rows, longest), jnp.bfloat16),
            pltpu.VMEM((slots, rows // 2, longest), jnp.bfloat16),
            pltpu.VMEM((slots, rows // 2, longest), jnp.bfloat16),
            pltpu.SemaphoreType.DMA((2,)),
            pltpu.SemaphoreType.DMA((slots,)),
            pltpu.SemaphoreType.DMA((slots, 2)),
        ],
        compiler_params=pltpu.CompilerParams(vmem_limit_bytes=56 * 1024 * 1024),
        cost_estimate=pl.CostEstimate(flops=1024, bytes_accessed=1024, transcendentals=0),
        name="prepare",
    )(me, owner, scales, values)
    return parts[: len(spans)], parts[len(spans) :], position


def apply_kernel(chosen, spans, block_width, projector_ref, position_ref, weights_ref, *refs):
    chain_count = len(spans)
    pieces = refs[: 4 * chain_count]
    out_hbm, reordered_ref, out_ref, out_sems = refs[-4:]
    rank = projector_ref.shape[1]
    runs = [
        (chain, at, size)
        for chain, (start, count) in enumerate(spans)
        for at, size in pieces_of(start, count)
    ]

    def outgoing(index):
        _, at, size = runs[index]
        slot = index % slots
        return pltpu.make_async_copy(
            out_ref.at[slot, :, pl.ds(0, size * block_width)],
            out_hbm.at[:, pl.ds(at * block_width, size * block_width)],
            out_sems.at[slot],
        )

    down = lax.broadcasted_iota(jnp.int32, (rank, rank), 0)
    for chain in range(chain_count):
        placing = (down == position_ref[chosen[chain]]).astype(jnp.bfloat16)
        reordered_ref[chain] = lax.dot_general(
            projector_ref[...],
            placing,
            (((1,), (1,)), ((), ())),
            preferred_element_type=jnp.float32,
        ).astype(jnp.bfloat16)
    for index, (chain, at, size) in enumerate(runs):
        slot = index % slots
        if index >= slots:
            outgoing(index - slots).wait()
        for block in range(0, size, 2):
            columns = slice(block * block_width, min(block + 2, size) * block_width)
            here = slice(columns.start + at * block_width, columns.stop + at * block_width)
            source = pl.ds(here.start - spans[chain][0] * block_width, here.stop - here.start)
            direction = jnp.concatenate(
                [piece[:, source] for piece in pieces[4 * chain : 4 * chain + 4]], axis=0
            )
            change = jnp.dot(reordered_ref[chain], direction, preferred_element_type=jnp.float32)
            out_ref[slot, :, columns] = (
                weights_ref[:, here].astype(jnp.float32) - update_scale * change
            ).astype(out_ref.dtype)
        outgoing(index).start()
    for index in range(max(0, len(runs) - slots), len(runs)):
        outgoing(index).wait()


def apply_update(projector, position, weights, pieces, so_far, chosen, spans, block_width):
    rows, rank = projector.shape
    longest = max(size for span in spans for _, size in pieces_of(*span)) * block_width
    whole = pl.BlockSpec(memory_space=pltpu.VMEM)
    anywhere = pl.BlockSpec(memory_space=pl.ANY)
    aliased = [] if so_far is None else [so_far]
    return pl.pallas_call(
        functools.partial(apply_kernel, chosen, spans, block_width),
        in_specs=[whole] * (3 + len(pieces)) + [anywhere] * len(aliased),
        out_specs=anywhere,
        input_output_aliases={3 + len(pieces): 0} if aliased else {},
        out_shape=jax.ShapeDtypeStruct(weights.shape, weights.dtype),
        scratch_shapes=[
            pltpu.VMEM((len(spans), rows, rank), jnp.bfloat16),
            pltpu.VMEM((slots, rows, longest), jnp.bfloat16),
            pltpu.SemaphoreType.DMA((slots,)),
        ],
        compiler_params=pltpu.CompilerParams(vmem_limit_bytes=20 * 1024 * 1024),
        cost_estimate=pl.CostEstimate(flops=1024, bytes_accessed=1024, transcendentals=0),
        name="apply_update",
    )(projector, position, weights, *pieces, *aliased)


def added(terms):
    return sum(term.astype(jnp.float32) for term in terms).astype(jnp.bfloat16)


def normalized(owned, first, second):
    new_first = first_decay * first + (1.0 - first_decay) * owned
    new_second = second_decay * second + (1.0 - second_decay) * owned * owned
    return new_first, new_second


def per_device(
    grad_values, grad_scales, block_owner, projector, weights, first_moment, second_moment
):
    shards, outers = lax.axis_size("shard"), lax.axis_size("outer")
    outer = lax.axis_index("outer")
    rank_rows = block_owner.shape[0]
    leaf_rows = rank_rows // shards // outers
    values = grad_values[0, 0]
    scales = grad_scales[0, 0].T
    col_blocks = scales.shape[0]
    block_width = values.shape[1] // col_blocks
    me = lax.axis_index(both).astype(jnp.int32)[None]

    turns = axis_orders()
    stages = len(turns[0])
    total = sum(share for share, _, _ in chains)
    ends = [
        round(col_blocks * sum(share for share, _, _ in chains[: i + 1]) / total)
        for i in range(len(chains))
    ]
    starts = [0] + ends[:-1]
    counts = [end - start for start, end in zip(starts, ends)]
    spans = list(zip(starts, counts))
    orders = [(turns[left], turns[right]) for _, left, right in chains]
    every = range(len(chains))

    last = [me]

    def turn_of(*arrays):
        return lax.optimization_barrier((*arrays, last[0]))[:-1]

    bits = [list(zip(*order)) for order in orders]
    partial, gathered, owned_parts = {}, {}, {}

    def reduce_stage(i, stage):
        mine, came = turn_of(*partial[i])
        half = mine.shape[0] // 2
        send = added([mine[half:], came[half:]])
        sent = swap(send, bits[i][stage])
        mine, came, last[0] = lax.optimization_barrier((mine, came, send))
        partial[i] = (added([mine[:half], came[:half]]), sent)

    def update_stage(i):
        owned_parts[i] = added(turn_of(*partial[i]))
        own = (outer * leaf_rows, starts[i] * block_width)
        shape = (leaf_rows, counts[i] * block_width)
        new_first, new_second = normalized(
            owned_parts[i].astype(jnp.float32),
            lax.dynamic_slice(first_moment, own, shape),
            lax.dynamic_slice(second_moment, own, shape),
        )
        corrected = new_first / (1.0 - first_decay**step_count)
        spread = jnp.sqrt(new_second / (1.0 - second_decay**step_count)) + 1e-08
        update = (corrected / spread).astype(jnp.bfloat16)
        gathered[i] = (update, swap(update, bits[i][-1]))
        last[0] = update

    def gather_stage(i, stage):
        mine = jnp.concatenate(turn_of(*gathered[i]), axis=0)
        gathered[i] = (mine, swap(mine, bits[i][stage]))
        last[0] = mine

    def owned_by_shard():
        owned = jnp.concatenate([owned_parts[i] for i in every], axis=1)
        for bit in bits_of(outers):
            other = swap(owned, (len(bits_of(shards)) + bit,) * 2)
            low = ((outer >> bit) & 1) == 0
            owned = jnp.where(
                low,
                jnp.concatenate([owned, other], axis=0),
                jnp.concatenate([other, owned], axis=0),
            )
        return owned

    def moments(owned):
        (owned,) = turn_of(owned)
        moved = normalized(owned.astype(jnp.float32), first_moment, second_moment)
        last[0] = moved[0]
        return moved

    keeps, sends, position = prepare(
        me, block_owner[None, :], values, scales, orders, spans, shards, leaf_rows
    )
    for i in every:
        partial[i] = [keeps[i], swap(sends[i], (0, 0))]
    owned = new_first = new_second = None
    work = [(stage + lags[i], i, stage) for i in every for stage in range(2 * stages)]
    for _, i, stage in sorted(work):
        if stage < stages:
            reduce_stage(i, stage)
        elif stage == stages:
            update_stage(i)
            if len(owned_parts) == len(chains):
                owned = owned_by_shard()
        else:
            if stage == 2 * stages - 1 and new_first is None:
                new_first, new_second = moments(owned)
            gather_stage(i, 2 * stages - 1 - stage)
    forwarded = {}
    for i in every:
        mine, came = gathered[i]
        beside = swap(mine, (0, 0))
        (came,) = turn_of(came)
        forwarded[i] = (mine, came, beside, swap(came, (0, 0)))
        last[0] = came
    new_weights = None
    for chosen in ((0, 1, 2), (3,)):
        new_weights = last[0] = apply_update(
            projector,
            position,
            weights,
            turn_of(*[piece for i in chosen for piece in forwarded[i]]),
            new_weights,
            chosen,
            [spans[i] for i in chosen],
            block_width,
        )
    return (new_weights, new_first, new_second)


def solution(mesh):
    placed = (
        P("outer", "shard", None, None),
        P("outer", "shard", None, None),
        P(),
        P(("outer", "shard"), None),
        P(("outer", "shard"), None),
        P("shard", None),
        P("shard", None),
    )
    return jax.shard_map(
        per_device,
        mesh=mesh,
        in_specs=placed,
        out_specs=(P(("outer", "shard"), None), P("shard", None), P("shard", None)),
        check_vma=False,
    )
```

```python
import functools

import jax
import jax.numpy as jnp
from jax import lax
from jax.experimental import pallas as pl
from jax.experimental.pallas import tpu as pltpu
from jax.sharding import PartitionSpec as P

first_decay = 0.9
second_decay = 0.999
step_count = 100.0
update_scale = 0.25
both = ("outer", "shard")
chains = ((1, 0, 1), (1, 2, 0), (1, 1, 2), (1, 0, 1))


runs_per_chain = 2
product_runs = 1
slots = 3
lags = (0, 0, 0, 0)


def bits_of(count):
    return list(range(count.bit_length() - 1))


def swap(array, bits):
    size = lax.axis_size("outer") * lax.axis_size("shard")
    return lax.ppermute(array, both, [(i, i ^ (1 << bits[i % 2])) for i in range(size)])


def axis_orders():
    shard_bits = bits_of(lax.axis_size("shard"))
    outer_bits = [len(shard_bits) + bit for bit in bits_of(lax.axis_size("outer"))]
    turning = shard_bits[1:2] + outer_bits + shard_bits[2:-1]
    return [turning[t:] + turning[:t] + shard_bits[-1:] for t in range(3)]


def pieces_of(start, count, run_count=None):
    run_count = run_count or runs_per_chain
    ends = [start + count * (run + 1) // run_count for run in range(run_count)]
    return [(at, end - at) for at, end in zip([start] + ends, ends) if end > at]


def prepare_kernel(spans, block_width, orders, shards, leaf_rows, me_ref, *refs):
    chain_count = len(spans)
    owner_hbm, scales_hbm, values_hbm = refs[:3]
    keep_refs, send_refs = refs[3 : 3 + chain_count], refs[3 + chain_count : 3 + 2 * chain_count]
    position_ref, owner_ref, scales_ref, wide_scales_ref, in_ref, keep_ref, send_ref = refs[
        3 + 2 * chain_count : -3
    ]
    small_sems, in_sems, out_sems = refs[-3:]
    rows = in_ref.shape[1]
    half = rows // 2
    runs = [
        (chain, at, size)
        for chain, (start, count) in enumerate(spans)
        for at, size in pieces_of(start, count)
    ]

    def incoming(index):
        _, at, size = runs[index]
        slot = index % slots
        return pltpu.make_async_copy(
            values_hbm.at[:, pl.ds(at * block_width, size * block_width)],
            in_ref.at[slot, :, pl.ds(0, size * block_width)],
            in_sems.at[slot],
        )

    def outgoing(index):
        chain, at, size = runs[index]
        slot = index % slots
        columns = pl.ds(0, size * block_width)
        target = pl.ds((at - spans[chain][0]) * block_width, size * block_width)
        return [
            pltpu.make_async_copy(
                buffer.at[slot, :, columns], outs[chain].at[:, target], out_sems.at[slot, which]
            )
            for which, (buffer, outs) in enumerate(((keep_ref, keep_refs), (send_ref, send_refs)))
        ]

    owner_copy = pltpu.make_async_copy(owner_hbm, owner_ref, small_sems.at[0])
    scales_copy = pltpu.make_async_copy(scales_hbm, scales_ref, small_sems.at[1])
    owner_copy.start()
    scales_copy.start()
    for index in range(min(slots - 1, len(runs))):
        incoming(index).start()
    owner_copy.wait()
    down = lax.broadcasted_iota(jnp.int32, (rows, rows), 0)
    across = lax.broadcasted_iota(jnp.int32, (rows, rows), 1)
    owner = owner_ref[...]
    owner_across = jnp.broadcast_to(owner, (rows, rows))
    earlier = (owner_across == owner_across.T) & (down < across)
    rank = jnp.sum(earlier.astype(jnp.int32), axis=0, keepdims=True)
    away = ((rank // leaf_rows) * shards + owner) ^ me_ref[0]
    for chain in range(chain_count):
        position = away & 1
        for bits in zip(*orders[chain]):
            bit = jnp.where(owner % 2 == 0, bits[0], bits[1])
            position = 2 * position + ((away >> bit) & 1)
        position_ref[chain] = position * leaf_rows + rank % leaf_rows
    scales_copy.wait()
    wide_scales_ref[...] = scales_ref[...].astype(jnp.float32)

    for index, (chain, at, size) in enumerate(runs):
        slot = index % slots
        if index + slots - 1 < len(runs):
            incoming(index + slots - 1).start()
        incoming(index).wait()
        if index >= slots:
            for copy in outgoing(index - slots):
                copy.wait()
        placing = (down == position_ref[chain]).astype(jnp.bfloat16)
        for block in range(size):
            columns = slice(block * block_width, (block + 1) * block_width)
            scale = wide_scales_ref[at + block : at + block + 1, :].astype(jnp.bfloat16)
            placed = jnp.dot(
                placing * scale, in_ref[slot, :, columns], preferred_element_type=jnp.float32
            ).astype(jnp.bfloat16)
            keep_ref[slot, :, columns] = placed[:half]
            send_ref[slot, :, columns] = placed[half:]
        for copy in outgoing(index):
            copy.start()
    for index in range(max(0, len(runs) - slots), len(runs)):
        for copy in outgoing(index):
            copy.wait()


def prepare(me, owner, values, scales, orders, spans, shards, leaf_rows):
    rows = values.shape[0]
    block_width = values.shape[1] // scales.shape[0]
    longest = max(size for span in spans for _, size in pieces_of(*span)) * block_width
    halves = [
        jax.ShapeDtypeStruct((rows // 2, count * block_width), jnp.bfloat16) for _, count in spans
    ]
    anywhere = pl.BlockSpec(memory_space=pl.ANY)
    *parts, position = pl.pallas_call(
        functools.partial(prepare_kernel, spans, block_width, orders, shards, leaf_rows),
        in_specs=[pl.BlockSpec(memory_space=pltpu.SMEM)] + [anywhere] * 3,
        out_specs=[anywhere] * (2 * len(spans)) + [pl.BlockSpec(memory_space=pltpu.VMEM)],
        out_shape=halves * 2 + [jax.ShapeDtypeStruct((len(spans), 1, rows), jnp.int32)],
        scratch_shapes=[
            pltpu.VMEM(owner.shape, jnp.int32),
            pltpu.VMEM(scales.shape, scales.dtype),
            pltpu.VMEM(scales.shape, jnp.float32),
            pltpu.VMEM((slots, rows, longest), jnp.bfloat16),
            pltpu.VMEM((slots, rows // 2, longest), jnp.bfloat16),
            pltpu.VMEM((slots, rows // 2, longest), jnp.bfloat16),
            pltpu.SemaphoreType.DMA((2,)),
            pltpu.SemaphoreType.DMA((slots,)),
            pltpu.SemaphoreType.DMA((slots, 2)),
        ],
        compiler_params=pltpu.CompilerParams(vmem_limit_bytes=56 * 1024 * 1024),
        cost_estimate=pl.CostEstimate(flops=1024, bytes_accessed=1024, transcendentals=0),
        name="prepare",
    )(me, owner, scales, values)
    return parts[: len(spans)], parts[len(spans) :], position


def apply_kernel(chosen, spans, block_width, projector_ref, position_ref, weights_ref, *refs):
    chain_count = len(spans)
    pieces = refs[: 4 * chain_count]
    out_hbm, reordered_ref, out_ref, out_sems = refs[-4:]
    rank = projector_ref.shape[1]
    runs = [
        (chain, at, size)
        for chain, (start, count) in enumerate(spans)
        for at, size in pieces_of(start, count, product_runs)
    ]

    def outgoing(index):
        _, at, size = runs[index]
        slot = index % slots
        return pltpu.make_async_copy(
            out_ref.at[slot, :, pl.ds(0, size * block_width)],
            out_hbm.at[:, pl.ds(at * block_width, size * block_width)],
            out_sems.at[slot],
        )

    down = lax.broadcasted_iota(jnp.int32, (rank, rank), 0)
    for chain in range(chain_count):
        placing = (down == position_ref[chosen[chain]]).astype(jnp.bfloat16)
        reordered_ref[chain] = lax.dot_general(
            projector_ref[...],
            placing,
            (((1,), (1,)), ((), ())),
            preferred_element_type=jnp.float32,
        ).astype(jnp.bfloat16)
    for index, (chain, at, size) in enumerate(runs):
        slot = index % slots
        if index >= slots:
            outgoing(index - slots).wait()
        for block in range(0, size, 4):
            columns = slice(block * block_width, min(block + 4, size) * block_width)
            here = slice(columns.start + at * block_width, columns.stop + at * block_width)
            source = pl.ds(here.start - spans[chain][0] * block_width, here.stop - here.start)
            direction = jnp.concatenate(
                [piece[:, source] for piece in pieces[4 * chain : 4 * chain + 4]], axis=0
            )
            change = jnp.dot(reordered_ref[chain], direction, preferred_element_type=jnp.float32)
            out_ref[slot, :, columns] = (
                weights_ref[:, here].astype(jnp.float32) - update_scale * change
            ).astype(out_ref.dtype)
        outgoing(index).start()
    for index in range(max(0, len(runs) - slots), len(runs)):
        outgoing(index).wait()


def apply_update(projector, position, weights, pieces, so_far, chosen, spans, block_width):
    rows, rank = projector.shape
    longest = max(size for span in spans for _, size in pieces_of(*span, product_runs)) * block_width
    whole = pl.BlockSpec(memory_space=pltpu.VMEM)
    anywhere = pl.BlockSpec(memory_space=pl.ANY)
    aliased = [] if so_far is None else [so_far]
    return pl.pallas_call(
        functools.partial(apply_kernel, chosen, spans, block_width),
        in_specs=[whole] * (3 + len(pieces)) + [anywhere] * len(aliased),
        out_specs=anywhere,
        input_output_aliases={3 + len(pieces): 0} if aliased else {},
        out_shape=jax.ShapeDtypeStruct(weights.shape, weights.dtype),
        scratch_shapes=[
            pltpu.VMEM((len(spans), rows, rank), jnp.bfloat16),
            pltpu.VMEM((slots, rows, longest), jnp.bfloat16),
            pltpu.SemaphoreType.DMA((slots,)),
        ],
        compiler_params=pltpu.CompilerParams(vmem_limit_bytes=20 * 1024 * 1024),
        cost_estimate=pl.CostEstimate(flops=1024, bytes_accessed=1024, transcendentals=0),
        name="apply_update",
    )(projector, position, weights, *pieces, *aliased)


def added(terms):
    return sum(term.astype(jnp.float32) for term in terms).astype(jnp.bfloat16)


def normalized(owned, first, second):
    new_first = first_decay * first + (1.0 - first_decay) * owned
    new_second = second_decay * second + (1.0 - second_decay) * owned * owned
    return new_first, new_second


def per_device(
    grad_values, grad_scales, block_owner, projector, weights, first_moment, second_moment
):
    shards, outers = lax.axis_size("shard"), lax.axis_size("outer")
    outer = lax.axis_index("outer")
    rank_rows = block_owner.shape[0]
    leaf_rows = rank_rows // shards // outers
    values = grad_values[0, 0]
    scales = grad_scales[0, 0].T
    col_blocks = scales.shape[0]
    block_width = values.shape[1] // col_blocks
    me = lax.axis_index(both).astype(jnp.int32)[None]

    turns = axis_orders()
    stages = len(turns[0])
    total = sum(share for share, _, _ in chains)
    ends = [
        round(col_blocks * sum(share for share, _, _ in chains[: i + 1]) / total)
        for i in range(len(chains))
    ]
    starts = [0] + ends[:-1]
    counts = [end - start for start, end in zip(starts, ends)]
    spans = list(zip(starts, counts))
    orders = [(turns[left], turns[right]) for _, left, right in chains]
    every = range(len(chains))

    last = [me]

    def turn_of(*arrays):
        return lax.optimization_barrier((*arrays, last[0]))[:-1]

    bits = [list(zip(*order)) for order in orders]
    partial, gathered, owned_parts = {}, {}, {}

    def reduce_stage(i, stage):
        mine, came = turn_of(*partial[i])
        half = mine.shape[0] // 2
        send = added([mine[half:], came[half:]])
        sent = swap(send, bits[i][stage])
        mine, came, last[0] = lax.optimization_barrier((mine, came, send))
        partial[i] = (added([mine[:half], came[:half]]), sent)

    def update_stage(i):
        owned_parts[i] = added(turn_of(*partial[i]))
        own = (outer * leaf_rows, starts[i] * block_width)
        shape = (leaf_rows, counts[i] * block_width)
        new_first, new_second = normalized(
            owned_parts[i].astype(jnp.float32),
            lax.dynamic_slice(first_moment, own, shape),
            lax.dynamic_slice(second_moment, own, shape),
        )
        corrected = new_first / (1.0 - first_decay**step_count)
        spread = jnp.sqrt(new_second / (1.0 - second_decay**step_count)) + 1e-08
        update = (corrected / spread).astype(jnp.bfloat16)
        gathered[i] = (update, swap(update, bits[i][-1]))
        last[0] = update

    def gather_stage(i, stage):
        mine = jnp.concatenate(turn_of(*gathered[i]), axis=0)
        gathered[i] = (mine, swap(mine, bits[i][stage]))
        last[0] = mine

    def owned_by_shard():
        owned = jnp.concatenate([owned_parts[i] for i in every], axis=1)
        for bit in bits_of(outers):
            other = swap(owned, (len(bits_of(shards)) + bit,) * 2)
            low = ((outer >> bit) & 1) == 0
            owned = jnp.where(
                low,
                jnp.concatenate([owned, other], axis=0),
                jnp.concatenate([other, owned], axis=0),
            )
        return owned

    def moments(owned):
        (owned,) = turn_of(owned)
        moved = normalized(owned.astype(jnp.float32), first_moment, second_moment)
        last[0] = moved[0]
        return moved

    keeps, sends, position = prepare(
        me, block_owner[None, :], values, scales, orders, spans, shards, leaf_rows
    )
    for i in every:
        partial[i] = [keeps[i], swap(sends[i], (0, 0))]
    owned = new_first = new_second = None
    work = [(stage + lags[i], i, stage) for i in every for stage in range(2 * stages)]
    for _, i, stage in sorted(work):
        if stage < stages:
            reduce_stage(i, stage)
        elif stage == stages:
            update_stage(i)
            if len(owned_parts) == len(chains):
                owned = owned_by_shard()
        else:
            if stage == 2 * stages - 1 and new_first is None:
                new_first, new_second = moments(owned)
            gather_stage(i, 2 * stages - 1 - stage)
    forwarded = {}
    for i in every:
        mine, came = gathered[i]
        beside = swap(mine, (0, 0))
        (came,) = turn_of(came)
        forwarded[i] = (mine, came, beside, swap(came, (0, 0)))
        last[0] = came
    new_weights = None
    for chosen in ((0, 1, 2), (3,)):
        new_weights = last[0] = apply_update(
            projector,
            position,
            weights,
            turn_of(*[piece for i in chosen for piece in forwarded[i]]),
            new_weights,
            chosen,
            [spans[i] for i in chosen],
            block_width,
        )
    return (new_weights, new_first, new_second)


def solution(mesh):
    placed = (
        P("outer", "shard", None, None),
        P("outer", "shard", None, None),
        P(),
        P(("outer", "shard"), None),
        P(("outer", "shard"), None),
        P("shard", None),
        P("shard", None),
    )
    return jax.shard_map(
        per_device,
        mesh=mesh,
        in_specs=placed,
        out_specs=(P(("outer", "shard"), None), P("shard", None), P("shard", None)),
        check_vma=False,
    )
```
